32 devices in a mesh: groups: 2 (over y), tile: 4 (over z), depth: 2 (over x), gx: 2 (over core).
Axes of the slice: x: 2, y: 2, z: 4, core: 2. Of those that a mesh axis runs over, the one named last changes fastest.
Arguments:
- frame_one: bfloat16 [128, 128, 256], P(('groups', 'depth'), 'tile', 'gx'), parts along dimension 0, may hold values from -6 to 6
- frame_two: bfloat16 [128, 128, 256], P(('groups', 'depth'), 'tile', 'gx'), parts along dimension 0, may hold values from -6 to 6
- shifts: int32 [3, 4, 4, 8], P(None, ('groups', 'depth'), 'tile', 'gx'), parts along dimension 1, may hold values from -1 to 7, as said below
Outputs:
- velocity: float32 [3, 128, 128, 256], P(None, ('groups', 'depth'), 'tile', 'gx'), parts along dimension 1
The draws below stay inside these ranges and needn't reach their ends.
There are 2 independent parts, one for each index of `groups`. The reference program is written for one: setup_inputs(seed, part) draws one part's arguments, and reference() takes and returns one part's arrays. A program takes and returns all parts, laid end to end along the dimension named above; each array names one. Nothing has to cross between parts.
Inputs may be any that keep to these rules, and one draw needn't show every extreme that they name: shifts[0] is -1, 0 or 1; shifts[1] lies in 0 to 3; shifts[2] lies in 0 to 7. The 4 blocks held by one device take their source blocks from exactly 2 distinct tiles of the y axis, 2 blocks from each.
All inputs are finite; a program needn't handle non-finite values.
Results may differ from the reference program's by a relative error of at most 0.0003.
Values may be sent and summed in bfloat16 or wider, within the bound.
A program may use at most 64 MiB of HBM per device.

```python
import jax
import jax.numpy as jnp
from jax import lax

BLK = 32
CX = 128
ITERS = 2
CY = 32
NZ = 64
NY = 128
NX = 256
BZ = 2
BY = 4
BX = 8


def draw_shifts(key, part):
    key = jax.random.fold_in(key, 11)
    tile_count = NY // CY
    x_count = CX // BLK
    per_device = x_count
    source_count = min(tile_count, per_device // 2)
    repeats = per_device // source_count
    depth_blocks = NZ // BLK
    row_blocks = NY // BLK
    column_blocks = NX // BLK
    device_count = depth_blocks * tile_count * 2
    subkeys = jax.random.split(key, 6)
    hot_rank = jax.random.permutation(subkeys[0], tile_count)
    favour = jnp.where(hot_rank < max(1, tile_count // 8), 1500, 0).astype(jnp.int32)
    random_part = jax.random.randint(subkeys[1], (device_count, tile_count), 0, 4096)
    scores = (random_part + favour[None, :]) * tile_count + jnp.arange(tile_count, dtype=jnp.int32)[None, :]
    unused, chosen = lax.top_k(scores, source_count)
    sources = jnp.repeat(chosen.astype(jnp.int32), repeats, axis=1)
    shuffle_keys = jax.random.randint(subkeys[2], (device_count, per_device), 0, 1 << 16) * per_device + jnp.arange(per_device, dtype=jnp.int32)[None, :]
    shuffle = jnp.argsort(shuffle_keys, axis=1)
    sources = jnp.take_along_axis(sources, shuffle, axis=1)
    depth_step = jax.random.randint(subkeys[4], (device_count, per_device), -1, 2)
    cross_step = jax.random.randint(subkeys[5], (device_count, per_device), 0, column_blocks)
    device_ids = jnp.arange(device_count, dtype=jnp.int32)
    tile_ids = device_ids // 2 % tile_count
    lateral_step = (sources - tile_ids[:, None]) % row_blocks
    stacked = jnp.stack([depth_step, lateral_step, cross_step]).astype(jnp.int32)
    return stacked.reshape(3, depth_blocks, row_blocks, column_blocks)


def block_scale(own_key, shape, pieces, smallest, largest):
    loudness = 1.0
    for axis_at, blocks in pieces:
        heights = jax.random.uniform(jax.random.fold_in(jax.random.fold_in(own_key, 6), axis_at), (blocks,), jnp.float32, smallest / len(pieces), largest / len(pieces))
        loudness = loudness * jnp.repeat(jnp.exp(heights), shape[axis_at] // blocks).reshape((-1,) + (1,) * (len(shape) - 1 - axis_at))
    return loudness


def noise(own_key, shape, scale, bound, cuts=(), held_as=jnp.bfloat16):
    factor_of = block_scale(own_key, shape, cuts, -0.22, 0.18) if cuts else 1.0
    entries = jax.random.normal(own_key, shape, jnp.float32) * scale * factor_of
    return jnp.minimum(jnp.maximum(entries, -bound), bound).astype(held_as)


def setup_inputs(seed: int = 0, part: int = 0) -> dict:
    seeds = jax.random.split(jax.random.key(seed), 4)
    own_keys = jax.random.split(jax.random.fold_in(seeds[3], part), 4)
    frame_one = noise(own_keys[0], (NZ, NY, NX), 1.0, 6.0, ((0, 2), (1, 4), (2, 2)))
    frame_two = noise(own_keys[1], (NZ, NY, NX), 1.0, 6.0, ((0, 2), (1, 4), (2, 2)))
    shifts = draw_shifts(jax.random.fold_in(jax.random.fold_in(seeds[3], part), 71), part)
    return dict(frame_one=frame_one, frame_two=frame_two, shifts=shifts)


SMOOTH = 1.0


def gradients(padded):
    first_frame = padded[0].astype(jnp.float32)
    second_frame = padded[1].astype(jnp.float32)
    bright = 0.5 * (first_frame + second_frame)
    grad_z = 0.5 * (bright[2:, 1:-1, 1:-1] - bright[:-2, 1:-1, 1:-1])
    grad_y = 0.5 * (bright[1:-1, 2:, 1:-1] - bright[1:-1, :-2, 1:-1])
    grad_x = 0.5 * (bright[1:-1, 1:-1, 2:] - bright[1:-1, 1:-1, :-2])
    change = (second_frame - first_frame)[1:-1, 1:-1, 1:-1]
    divisor = SMOOTH + grad_z * grad_z + grad_y * grad_y + grad_x * grad_x
    return grad_z, grad_y, grad_x, change, divisor


def sweep(rimmed, coeffs):
    grad_z, grad_y, grad_x, change, divisor = coeffs
    average = (rimmed[:, 2:, 1:-1, 1:-1] + rimmed[:, :-2, 1:-1, 1:-1] + rimmed[:, 1:-1, 2:, 1:-1]
               + rimmed[:, 1:-1, :-2, 1:-1] + rimmed[:, 1:-1, 1:-1, 2:] + rimmed[:, 1:-1, 1:-1, :-2]) / 6.0
    residual = (grad_z * average[0] + grad_y * average[1] + grad_x * average[2] + change) / divisor
    return jnp.stack([average[0] - grad_z * residual, average[1] - grad_y * residual, average[2] - grad_x * residual])


def reference(frame_one, frame_two, shifts):
    blocks_view = frame_two.reshape(BZ, BLK, BY, BLK, BX, BLK).transpose(0, 2, 4, 1, 3, 5)
    depth_ids = jnp.arange(BZ, dtype=jnp.int32)[:, None, None]
    row_ids = jnp.arange(BY, dtype=jnp.int32)[None, :, None]
    column_ids = jnp.arange(BX, dtype=jnp.int32)[None, None, :]
    source_z = (depth_ids + shifts[0]) % BZ
    source_y = (row_ids + shifts[1]) % BY
    source_x = (column_ids + shifts[2]) % BX
    moved_blocks = blocks_view[source_z, source_y, source_x]
    warped = moved_blocks.transpose(0, 3, 1, 4, 2, 5).reshape(NZ, NY, NX)
    frame_pair = jnp.pad(jnp.stack([frame_one, warped]), ((0, 0), (1, 1), (1, 1), (1, 1)))
    coeffs = gradients(frame_pair)
    velocity = jnp.zeros((3, NZ, NY, NX), jnp.float32)
    for sweep_index in range(ITERS):
        velocity = sweep(jnp.pad(velocity, ((0, 0), (1, 1), (1, 1), (1, 1))), coeffs)
    return velocity
```

```python
import functools

import jax
import jax.numpy as jnp
from jax import lax
from jax.experimental import pallas as pl
from jax.experimental.pallas import tpu as pltpu
from jax.sharding import PartitionSpec as P

MESH = pl.DeviceIdType.MESH
F32 = jnp.float32
BF16 = jnp.bfloat16
E = 32
L = 128
NB = 4
CAP = 2
PK = 8
PAD = 8
CHUNKS = 2


def regroup(rows, lane):
    a, b, c, d = rows
    low = lane < 64
    r64 = lambda v: pltpu.roll(v, 64, 1)
    a, c = jnp.where(low, a, r64(c)), jnp.where(low, r64(a), c)
    b, d = jnp.where(low, b, r64(d)), jnp.where(low, r64(b), d)
    even = lax.rem(lane, 64) < 32
    a, b = (jnp.where(even, a, pltpu.roll(b, 32, 1)), jnp.where(even, pltpu.roll(a, 96, 1), b))
    c, d = (jnp.where(even, c, pltpu.roll(d, 32, 1)), jnp.where(even, pltpu.roll(c, 96, 1), d))
    return [a, b, c, d]


def kernel(T, Z, f1, f2, sh, out, *scr):
    C = CHUNKS
    S, scr = scr[:C], scr[C:]
    A, scr = scr[:C], scr[C:]
    (B, shr, shs, brp, chs, g, inv, v1p, yb, xb, yv, xv, ybs, xbs, yvs, xvs,
     sem_sh_s, sem_sh_r, sem_loc, sem_gx_s, sem_gx_r, sem_d_s, sem_d_r, sem_f_s, sem_f_r,
     sem_t_s, sem_t_r, sem_h_s, sem_h_r, sem_v_s, sem_v_r) = scr
    CP = PK // C
    m = lax.axis_index("tile")
    z = lax.axis_index("depth")
    x = lax.axis_index("gx")
    px = 1 - x
    nslots = min(Z, 3)
    steps = {1: [], 2: [1]}.get(Z, [1, Z - 1])

    def rcopy(src, dst, ss, rs, dev):
        return pltpu.make_async_remote_copy(
            src_ref=src, dst_ref=dst, send_sem=ss, recv_sem=rs, device_id=dev, device_id_type=MESH)

    barrier = pltpu.get_barrier_semaphore()
    for o in range(1, T):
        pl.semaphore_signal(barrier, inc=1, device_id={"tile": lax.rem(m + o, T)}, device_id_type=MESH)
    for st in steps:
        pl.semaphore_signal(barrier, inc=1, device_id={"depth": lax.rem(z + st, Z)}, device_id_type=MESH)
    pl.semaphore_signal(barrier, inc=1, device_id={"gx": px}, device_id_type=MESH)

    lane = lax.broadcasted_iota(jnp.int32, (E, L), 1)

    for c in range(C):
        def pack(zz, carry, c=c):
            rows = [f2[c * CP + zz + PK * q].astype(F32) for q in range(NB)]
            for b, v in enumerate(regroup(rows, lane)):
                S[c][b, zz] = v.astype(BF16)
            return carry
        lax.fori_loop(0, CP, pack, 0)
    shr[m] = sh[...]

    pl.semaphore_wait(barrier, T - 1 + len(steps) + 1)

    sh_cp = []
    for o in range(1, T):
        t = lax.rem(m + o, T)
        cp = rcopy(sh, shr.at[m], sem_sh_s.at[o], sem_sh_r.at[o], {"tile": t})
        cp.start()
        sh_cp.append(cp)

    gx_cp, d_cp = [], []
    for c in range(C):
        own = S[c].at[pl.ds(0, NB)]
        dl = []
        for k, st in enumerate(steps):
            slot = 1 + (k if Z == 2 else 1 - k)
            cp = rcopy(own, S[c].at[pl.ds(slot * 2 * NB, NB)], sem_d_s.at[c, k], sem_d_r.at[c, k],
                       {"depth": lax.rem(z + st, Z)})
            cp.start()
            dl.append((cp, slot))
        d_cp.append(dl)
    for c in range(C):
        cp = rcopy(S[c].at[pl.ds(0, NB)], S[c].at[pl.ds(NB, NB)], sem_gx_s.at[c], sem_gx_r.at[c], {"gx": px})
        cp.start()
        gx_cp.append(cp)

    for cp in sh_cp:
        cp.wait_recv()
    loc = pltpu.make_async_copy(shr, shs, sem_loc)
    loc.start()
    loc.wait()

    def sources(t):
        tiles = [lax.rem(t + shs[t, 1, b], T) for b in range(NB)]
        ranks = []
        for b in range(NB):
            r = jnp.int32(0)
            for e in range(b):
                r = r + jnp.where(tiles[e] == tiles[b], 1, 0)
            ranks.append(r)
        return tiles, ranks

    def rows_for(t):
        tiles, ranks = sources(t)
        picked = [jnp.int32(0)] * CAP
        for b in range(NB):
            s0 = shs[t, 0, b]
            if Z == 1:
                slot = jnp.int32(0)
            elif Z == 2:
                slot = s0 * s0
            else:
                slot = jnp.where(s0 < 0, 2, s0)
            row = slot * (2 * NB) + lax.rem(b + shs[t, 2, b], 2 * NB)
            for k in range(CAP):
                hit = (tiles[b] == m) & (ranks[b] == k)
                picked[k] = picked[k] + jnp.where(hit, row, 0)
        return picked

    want = [rows_for(lax.rem(m + o, T)) for o in range(T)]

    f_cp = []
    t_cp = []
    for c in range(C):
        gx_cp[c].wait_recv()
        fl = []
        for k, (cp, slot) in enumerate(d_cp[c]):
            cp.wait_recv()
            at = slot * 2 * NB
            f = rcopy(S[c].at[pl.ds(at, NB)], S[c].at[pl.ds(at + NB, NB)],
                      sem_f_s.at[c, k], sem_f_r.at[c, k], {"gx": px})
            f.start()
            fl.append(f)
        for f in fl:
            f.wait_recv()
        f_cp.append(fl)
        tl = []
        for o in list(range(1, T)) + [0]:
            t = lax.rem(m + o, T)
            for k in range(CAP):
                row = want[o][k]

                def cut(zz, carry, c=c, o=o, k=k, row=row):
                    if o == 0:
                        A[c][m * CAP + k, zz] = S[c][row, zz]
                    else:
                        B[c, o, k, zz] = S[c][row, zz]
                    return carry
                lax.fori_loop(0, CP, cut, 0)
            if o:
                cp = rcopy(B.at[c, o], A[c].at[pl.ds(m * CAP, CAP)], sem_t_s.at[c, o], sem_t_r.at[c, o], {"tile": t})
                cp.start()
                tl.append(cp)
        t_cp.append(tl)

    tiles, ranks = sources(m)
    pick = [tiles[b] * CAP + jnp.minimum(ranks[b], CAP - 1) for b in range(NB)]
    src_lane = jnp.where(x == 0, L - 1, 0)
    dst_lane = src_lane
    body = pl.ds(PAD, E)

    xbs[...] = jnp.zeros((E, L), F32)
    for c in range(C):
        for cp in t_cp[c]:
            cp.wait_recv()

        def unpack(zz, carry, c=c):
            rows = [A[c][pick[b], zz].astype(F32) for b in range(NB)]
            for q, w in enumerate(regroup(rows, lane)):
                zi = c * CP + zz + PK * q
                one = f1[zi].astype(F32)
                br = 0.5 * (one + w)
                brp[zi + 1, body] = br
                chs[zi] = w - one
                ybs[0, pl.ds(zi, 1)] = br[0:1]
                ybs[1, pl.ds(zi, 1)] = br[E - 1:E]
                col = pltpu.roll(br, lax.rem(zi - src_lane + L, L), 1)
                xbs[...] = jnp.where(lane == zi, col, xbs[...])
            return carry
        lax.fori_loop(0, CP, unpack, 0)

    def faces(zlo_src, zhi_src, zlo_dst, zhi_dst, ys, yr, xs, xr, ss, rs):
        plan = [
            (ys[1], yr[0], 0, m < T - 1, m > 0, {"tile": jnp.minimum(m + 1, T - 1)}),
            (ys[0], yr[1], 1, m > 0, m < T - 1, {"tile": jnp.maximum(m - 1, 0)}),
            (zhi_src, zlo_dst, 2, z < Z - 1, z > 0, {"depth": jnp.minimum(z + 1, Z - 1)}),
            (zlo_src, zhi_dst, 3, z > 0, z < Z - 1, {"depth": jnp.maximum(z - 1, 0)}),
        ]
        cx = rcopy(xs, xr, ss.at[4], rs.at[4], {"gx": px})
        todo = []
        for src, dst, i, has_to, has_from, dev in plan:
            cp = rcopy(src, dst, ss.at[i], rs.at[i], dev)

            @pl.when(has_to)
            def _():
                cp.start()

            @pl.when(jnp.logical_not(has_from))
            def _():
                dst[...] = jnp.zeros(dst.shape, F32)
            todo.append((cp, has_to, has_from))
        cx.start()

        def wait_recv():
            for cp, has_to, has_from in todo:
                @pl.when(has_from)
                def _():
                    cp.wait_recv()
            cx.wait_recv()

        def wait_send():
            for cp, has_to, has_from in todo:
                @pl.when(has_to)
                def _():
                    cp.wait_send()
            cx.wait_send()
        return wait_recv, wait_send

    wr1, ws1 = faces(brp.at[1, body], brp.at[E, body], brp.at[0, body], brp.at[E + 1, body],
                     [ybs.at[0], ybs.at[1]], [yb.at[0], yb.at[1]], xbs, xb, sem_h_s, sem_h_r)
    wr1()

    is0 = jnp.where(x == 0, 1.0, 0.0).astype(F32)
    is1 = 1.0 - is0

    def x_pair(v, halo):
        nxt = jnp.where(lane == L - 1, halo * is0, pltpu.roll(v, L - 1, 1))
        prv = jnp.where(lane == 0, halo * is1, pltpu.roll(v, 1, 1))
        return nxt, prv

    for i in range(3):
        xvs[i] = jnp.zeros((E, L), F32)

    def first(zi, carry):
        back = lax.rem(dst_lane - zi + L, L)
        brp[zi + 1, pl.ds(PAD - 1, 1)] = yb[0, pl.ds(zi, 1)]
        brp[zi + 1, pl.ds(PAD + E, 1)] = yb[1, pl.ds(zi, 1)]
        br = brp[zi + 1, body]
        gz = 0.5 * (brp[zi + 2, body] - brp[zi, body])
        gy = 0.5 * (brp[zi + 1, pl.ds(PAD + 1, E)] - brp[zi + 1, pl.ds(PAD - 1, E)])
        nxt, prv = x_pair(br, pltpu.roll(xb[...], back, 1))
        gx = 0.5 * (nxt - prv)
        iv = 1.0 / (1.0 + gz * gz + gy * gy + gx * gx)
        res = chs[zi] * iv
        inv[zi] = iv
        move = lax.rem(zi - src_lane + L, L)
        for i, gg in enumerate((gz, gy, gx)):
            g[i, zi] = gg
            v = -gg * res
            v1p[i, zi + 1, body] = v
            yvs[0, i, pl.ds(zi, 1)] = v[0:1]
            yvs[1, i, pl.ds(zi, 1)] = v[E - 1:E]
            xvs[i] = jnp.where(lane == zi, pltpu.roll(v, move, 1), xvs[i])
        return carry
    lax.fori_loop(0, E, first, 0)

    three = pl.ds(0, 3)
    wr2, ws2 = faces(v1p.at[three, 1, body], v1p.at[three, E, body], v1p.at[three, 0, body], v1p.at[three, E + 1, body],
                     [yvs.at[0], yvs.at[1]], [yv.at[0], yv.at[1]], xvs, xv, sem_v_s, sem_v_r)
    wr2()

    def second(zi, carry):
        back = lax.rem(dst_lane - zi + L, L)
        avg = []
        for i in range(3):
            v1p[i, zi + 1, pl.ds(PAD - 1, 1)] = yv[0, i, pl.ds(zi, 1)]
            v1p[i, zi + 1, pl.ds(PAD + E, 1)] = yv[1, i, pl.ds(zi, 1)]
            v = v1p[i, zi + 1, body]
            nxt, prv = x_pair(v, pltpu.roll(xv[i], back, 1))
            total = (v1p[i, zi + 2, body] + v1p[i, zi, body]
                     + v1p[i, zi + 1, pl.ds(PAD + 1, E)] + v1p[i, zi + 1, pl.ds(PAD - 1, E)] + nxt + prv)
            avg.append(total * (1.0 / 6.0))
        gs = [g[i, zi] for i in range(3)]
        res = (gs[0] * avg[0] + gs[1] * avg[1] + gs[2] * avg[2] + chs[zi]) * inv[zi]
        for i in range(3):
            out[i, zi] = avg[i] - gs[i] * res
        return carry
    lax.fori_loop(0, E, second, 0)

    for cp in sh_cp:
        cp.wait_send()
    for c in range(C):
        gx_cp[c].wait_send()
        for cp, slot in d_cp[c]:
            cp.wait_send()
        for cp in f_cp[c]:
            cp.wait_send()
        for cp in t_cp[c]:
            cp.wait_send()
    ws1()
    ws2()


def local(T, Z, frame_one, frame_two, shifts):
    C = CHUNKS
    CP = PK // C
    own = jnp.pad(shifts.reshape(3, NB), ((0, 5), (0, L - NB)))
    nslots = min(Z, 3)
    dma = pltpu.SemaphoreType.DMA
    ns = max(1, nslots - 1)
    vm = pltpu.VMEM
    scratch = [vm((nslots * 2 * NB, CP, E, L), BF16) for _ in range(C)]
    scratch += [vm((T * CAP, CP, E, L), BF16) for _ in range(C)]
    scratch += [
        vm((C, T, CAP, CP, E, L), BF16),
        vm((T, 8, L), jnp.int32),
        pltpu.SMEM((T, 8, L), jnp.int32),
        vm((E + 2, E + 2 * PAD, L), F32),
        vm((E, E, L), F32),
        vm((3, E, E, L), F32),
        vm((E, E, L), F32),
        vm((3, E + 2, E + 2 * PAD, L), F32),
        vm((2, E, L), F32), vm((E, L), F32), vm((2, 3, E, L), F32), vm((3, E, L), F32),
        vm((2, E, L), F32), vm((E, L), F32), vm((2, 3, E, L), F32), vm((3, E, L), F32),
        dma((T,)), dma((T,)), dma, dma((C,)), dma((C,)),
        dma((C, ns)), dma((C, ns)), dma((C, ns)), dma((C, ns)),
        dma((C, T)), dma((C, T)), dma((5,)), dma((5,)), dma((5,)), dma((5,)),
    ]
    return pl.pallas_call(
        functools.partial(kernel, T, Z),
        out_shape=jax.ShapeDtypeStruct((3,) + frame_one.shape, F32),
        in_specs=[pl.BlockSpec(memory_space=pltpu.VMEM)] * 3,
        out_specs=pl.BlockSpec(memory_space=pltpu.VMEM),
        scratch_shapes=scratch,
        compiler_params=pltpu.CompilerParams(
            collective_id=0, has_side_effects=True, vmem_limit_bytes=40 * 1024 * 1024),
        cost_estimate=pl.CostEstimate(flops=131072 * 60, bytes_accessed=2 << 20, transcendentals=0),
        name="warp_flow",
    )(frame_one, frame_two, own)


def solution(mesh):
    spec = P(("groups", "depth"), "tile", "gx")
    vec = P(None, ("groups", "depth"), "tile", "gx")
    body = functools.partial(local, mesh.shape["tile"], mesh.shape["depth"])
    return jax.shard_map(body, mesh=mesh, in_specs=(spec, spec, vec), out_specs=vec, check_vma=False)
```

```python
import functools

import jax
import jax.numpy as jnp
from jax import lax
from jax.experimental import pallas as pl
from jax.experimental.pallas import tpu as pltpu
from jax.sharding import PartitionSpec as P

MESH = pl.DeviceIdType.MESH
F32 = jnp.float32
BF16 = jnp.bfloat16
E = 32
L = 128
NB = 4
CAP = 2
PK = 8
PAD = 8
CHUNKS = 2


def regroup(rows, lane):
    a, b, c, d = rows
    low = lane < 64
    r64 = lambda v: pltpu.roll(v, 64, 1)
    a, c = jnp.where(low, a, r64(c)), jnp.where(low, r64(a), c)
    b, d = jnp.where(low, b, r64(d)), jnp.where(low, r64(b), d)
    even = lax.rem(lane, 64) < 32
    a, b = (jnp.where(even, a, pltpu.roll(b, 32, 1)), jnp.where(even, pltpu.roll(a, 96, 1), b))
    c, d = (jnp.where(even, c, pltpu.roll(d, 32, 1)), jnp.where(even, pltpu.roll(c, 96, 1), d))
    return [a, b, c, d]


def kernel(T, Z, f1_hbm, f2_hbm, sh, out, *scr):
    C = CHUNKS
    S, scr = scr[:C], scr[C:]
    A, scr = scr[:C], scr[C:]
    (B, shr, shs, brp, chs, g, inv, v1p, yb, xb, yv, xv, ybs, xbs, yvs, xvs,
     sem_sh_s, sem_sh_r, sem_loc, sem_gx_s, sem_gx_r, sem_d_s, sem_d_r, sem_f_s, sem_f_r,
     sem_t_s, sem_t_r, sem_h_s, sem_h_r, sem_v_s, sem_v_r, f1, f2, sem_in) = scr
    in2 = pltpu.make_async_copy(f2_hbm, f2, sem_in.at[0])
    in2.start()
    in1 = pltpu.make_async_copy(f1_hbm, f1, sem_in.at[1])
    in1.start()
    CP = PK // C
    m = lax.axis_index("tile")
    z = lax.axis_index("depth")
    x = lax.axis_index("gx")
    px = 1 - x
    nslots = min(Z, 3)
    steps = {1: [], 2: [1]}.get(Z, [1, Z - 1])

    def rcopy(src, dst, ss, rs, dev):
        return pltpu.make_async_remote_copy(
            src_ref=src, dst_ref=dst, send_sem=ss, recv_sem=rs, device_id=dev, device_id_type=MESH)

    barrier = pltpu.get_barrier_semaphore()
    for o in range(1, T):
        pl.semaphore_signal(barrier, inc=1, device_id={"tile": lax.rem(m + o, T)}, device_id_type=MESH)
    for st in steps:
        pl.semaphore_signal(barrier, inc=1, device_id={"depth": lax.rem(z + st, Z)}, device_id_type=MESH)
    pl.semaphore_signal(barrier, inc=1, device_id={"gx": px}, device_id_type=MESH)

    lane = lax.broadcasted_iota(jnp.int32, (E, L), 1)

    in2.wait()
    for c in range(C):
        def pack(zz, carry, c=c):
            rows = [f2[c * CP + zz + PK * q].astype(F32) for q in range(NB)]
            for b, v in enumerate(regroup(rows, lane)):
                S[c][b, zz] = v.astype(BF16)
            return carry
        lax.fori_loop(0, CP, pack, 0)
    shr[m] = sh[...]

    pl.semaphore_wait(barrier, T - 1 + len(steps) + 1)

    sh_cp = []
    for o in range(1, T):
        t = lax.rem(m + o, T)
        cp = rcopy(sh, shr.at[m], sem_sh_s.at[o], sem_sh_r.at[o], {"tile": t})
        cp.start()
        sh_cp.append(cp)

    gx_cp, d_cp = [], []
    for c in range(C):
        own = S[c].at[pl.ds(0, NB)]
        dl = []
        for k, st in enumerate(steps):
            slot = 1 + (k if Z == 2 else 1 - k)
            cp = rcopy(own, S[c].at[pl.ds(slot * 2 * NB, NB)], sem_d_s.at[c, k], sem_d_r.at[c, k],
                       {"depth": lax.rem(z + st, Z)})
            cp.start()
            dl.append((cp, slot))
        d_cp.append(dl)
    for c in range(C):
        cp = rcopy(S[c].at[pl.ds(0, NB)], S[c].at[pl.ds(NB, NB)], sem_gx_s.at[c], sem_gx_r.at[c], {"gx": px})
        cp.start()
        gx_cp.append(cp)

    for cp in sh_cp:
        cp.wait_recv()
    loc = pltpu.make_async_copy(shr, shs, sem_loc)
    loc.start()
    loc.wait()

    def sources(t):
        tiles = [lax.rem(t + shs[t, 1, b], T) for b in range(NB)]
        ranks = []
        for b in range(NB):
            r = jnp.int32(0)
            for e in range(b):
                r = r + jnp.where(tiles[e] == tiles[b], 1, 0)
            ranks.append(r)
        return tiles, ranks

    def rows_for(t):
        tiles, ranks = sources(t)
        picked = [jnp.int32(0)] * CAP
        for b in range(NB):
            s0 = shs[t, 0, b]
            if Z == 1:
                slot = jnp.int32(0)
            elif Z == 2:
                slot = s0 * s0
            else:
                slot = jnp.where(s0 < 0, 2, s0)
            row = slot * (2 * NB) + lax.rem(b + shs[t, 2, b], 2 * NB)
            for k in range(CAP):
                hit = (tiles[b] == m) & (ranks[b] == k)
                picked[k] = picked[k] + jnp.where(hit, row, 0)
        return picked

    want = [rows_for(lax.rem(m + o, T)) for o in range(T)]

    f_cp = []
    t_cp = []
    for c in range(C):
        gx_cp[c].wait_recv()
        fl = []
        for k, (cp, slot) in enumerate(d_cp[c]):
            cp.wait_recv()
            at = slot * 2 * NB
            f = rcopy(S[c].at[pl.ds(at, NB)], S[c].at[pl.ds(at + NB, NB)],
                      sem_f_s.at[c, k], sem_f_r.at[c, k], {"gx": px})
            f.start()
            fl.append(f)
        for f in fl:
            f.wait_recv()
        f_cp.append(fl)
        tl = []
        for o in list(range(1, T)) + [0]:
            t = lax.rem(m + o, T)
            for k in range(CAP):
                row = want[o][k]

                def cut(zz, carry, c=c, o=o, k=k, row=row):
                    if o == 0:
                        A[c][m * CAP + k, zz] = S[c][row, zz]
                    else:
                        B[c, o, k, zz] = S[c][row, zz]
                    return carry
                lax.fori_loop(0, CP, cut, 0)
            if o:
                cp = rcopy(B.at[c, o], A[c].at[pl.ds(m * CAP, CAP)], sem_t_s.at[c, o], sem_t_r.at[c, o], {"tile": t})
                cp.start()
                tl.append(cp)
        t_cp.append(tl)

    tiles, ranks = sources(m)
    pick = [tiles[b] * CAP + jnp.minimum(ranks[b], CAP - 1) for b in range(NB)]
    src_lane = jnp.where(x == 0, L - 1, 0)
    dst_lane = src_lane
    body = pl.ds(PAD, E)

    xbs[...] = jnp.zeros((E, L), F32)
    in1.wait()
    for c in range(C):
        for cp in t_cp[c]:
            cp.wait_recv()

        def unpack(zz, carry, c=c):
            rows = [A[c][pick[b], zz].astype(F32) for b in range(NB)]
            for q, w in enumerate(regroup(rows, lane)):
                zi = c * CP + zz + PK * q
                one = f1[zi].astype(F32)
                br = 0.5 * (one + w)
                brp[zi + 1, body] = br
                chs[zi] = w - one
                ybs[0, pl.ds(zi, 1)] = br[0:1]
                ybs[1, pl.ds(zi, 1)] = br[E - 1:E]
                col = pltpu.roll(br, lax.rem(zi - src_lane + L, L), 1)
                xbs[...] = jnp.where(lane == zi, col, xbs[...])
            return carry
        lax.fori_loop(0, CP, unpack, 0)

    def faces(zlo_src, zhi_src, zlo_dst, zhi_dst, ys, yr, xs, xr, ss, rs):
        plan = [
            (ys[1], yr[0], 0, m < T - 1, m > 0, {"tile": jnp.minimum(m + 1, T - 1)}),
            (ys[0], yr[1], 1, m > 0, m < T - 1, {"tile": jnp.maximum(m - 1, 0)}),
            (zhi_src, zlo_dst, 2, z < Z - 1, z > 0, {"depth": jnp.minimum(z + 1, Z - 1)}),
            (zlo_src, zhi_dst, 3, z > 0, z < Z - 1, {"depth": jnp.maximum(z - 1, 0)}),
        ]
        cx = rcopy(xs, xr, ss.at[4], rs.at[4], {"gx": px})
        todo = []
        for src, dst, i, has_to, has_from, dev in plan:
            cp = rcopy(src, dst, ss.at[i], rs.at[i], dev)

            @pl.when(has_to)
            def _():
                cp.start()

            @pl.when(jnp.logical_not(has_from))
            def _():
                dst[...] = jnp.zeros(dst.shape, F32)
            todo.append((cp, has_to, has_from))
        cx.start()

        def wait_recv():
            for cp, has_to, has_from in todo:
                @pl.when(has_from)
                def _():
                    cp.wait_recv()
            cx.wait_recv()

        def wait_send():
            for cp, has_to, has_from in todo:
                @pl.when(has_to)
                def _():
                    cp.wait_send()
            cx.wait_send()
        return wait_recv, wait_send

    wr1, ws1 = faces(brp.at[1, body], brp.at[E, body], brp.at[0, body], brp.at[E + 1, body],
                     [ybs.at[0], ybs.at[1]], [yb.at[0], yb.at[1]], xbs, xb, sem_h_s, sem_h_r)
    wr1()

    is0 = jnp.where(x == 0, 1.0, 0.0).astype(F32)
    is1 = 1.0 - is0

    def x_pair(v, halo):
        nxt = jnp.where(lane == L - 1, halo * is0, pltpu.roll(v, L - 1, 1))
        prv = jnp.where(lane == 0, halo * is1, pltpu.roll(v, 1, 1))
        return nxt, prv

    for i in range(3):
        xvs[i] = jnp.zeros((E, L), F32)

    def first(zi, carry):
        back = lax.rem(dst_lane - zi + L, L)
        brp[zi + 1, pl.ds(PAD - 1, 1)] = yb[0, pl.ds(zi, 1)]
        brp[zi + 1, pl.ds(PAD + E, 1)] = yb[1, pl.ds(zi, 1)]
        br = brp[zi + 1, body]
        gz = 0.5 * (brp[zi + 2, body] - brp[zi, body])
        gy = 0.5 * (brp[zi + 1, pl.ds(PAD + 1, E)] - brp[zi + 1, pl.ds(PAD - 1, E)])
        nxt, prv = x_pair(br, pltpu.roll(xb[...], back, 1))
        gx = 0.5 * (nxt - prv)
        iv = 1.0 / (1.0 + gz * gz + gy * gy + gx * gx)
        res = chs[zi] * iv
        inv[zi] = iv
        move = lax.rem(zi - src_lane + L, L)
        for i, gg in enumerate((gz, gy, gx)):
            g[i, zi] = gg
            v = -gg * res
            v1p[i, zi + 1, body] = v
            yvs[0, i, pl.ds(zi, 1)] = v[0:1]
            yvs[1, i, pl.ds(zi, 1)] = v[E - 1:E]
            xvs[i] = jnp.where(lane == zi, pltpu.roll(v, move, 1), xvs[i])
        return carry
    lax.fori_loop(0, E, first, 0, unroll=4)

    three = pl.ds(0, 3)
    wr2, ws2 = faces(v1p.at[three, 1, body], v1p.at[three, E, body], v1p.at[three, 0, body], v1p.at[three, E + 1, body],
                     [yvs.at[0], yvs.at[1]], [yv.at[0], yv.at[1]], xvs, xv, sem_v_s, sem_v_r)
    wr2()

    def second(zi, carry):
        back = lax.rem(dst_lane - zi + L, L)
        avg = []
        for i in range(3):
            v1p[i, zi + 1, pl.ds(PAD - 1, 1)] = yv[0, i, pl.ds(zi, 1)]
            v1p[i, zi + 1, pl.ds(PAD + E, 1)] = yv[1, i, pl.ds(zi, 1)]
            v = v1p[i, zi + 1, body]
            nxt, prv = x_pair(v, pltpu.roll(xv[i], back, 1))
            total = (v1p[i, zi + 2, body] + v1p[i, zi, body]
                     + v1p[i, zi + 1, pl.ds(PAD + 1, E)] + v1p[i, zi + 1, pl.ds(PAD - 1, E)] + nxt + prv)
            avg.append(total * (1.0 / 6.0))
        gs = [g[i, zi] for i in range(3)]
        res = (gs[0] * avg[0] + gs[1] * avg[1] + gs[2] * avg[2] + chs[zi]) * inv[zi]
        for i in range(3):
            out[i, zi] = avg[i] - gs[i] * res
        return carry
    lax.fori_loop(0, E, second, 0, unroll=4)

    for cp in sh_cp:
        cp.wait_send()
    for c in range(C):
        gx_cp[c].wait_send()
        for cp, slot in d_cp[c]:
            cp.wait_send()
        for cp in f_cp[c]:
            cp.wait_send()
        for cp in t_cp[c]:
            cp.wait_send()
    ws1()
    ws2()


def local(T, Z, frame_one, frame_two, shifts):
    C = CHUNKS
    CP = PK // C
    own = jnp.pad(shifts.reshape(3, NB), ((0, 5), (0, L - NB)))
    nslots = min(Z, 3)
    dma = pltpu.SemaphoreType.DMA
    ns = max(1, nslots - 1)
    vm = pltpu.VMEM
    scratch = [vm((nslots * 2 * NB, CP, E, L), BF16) for _ in range(C)]
    scratch += [vm((T * CAP, CP, E, L), BF16) for _ in range(C)]
    scratch += [
        vm((C, T, CAP, CP, E, L), BF16),
        vm((T, 8, L), jnp.int32),
        pltpu.SMEM((T, 8, L), jnp.int32),
        vm((E + 2, E + 2 * PAD, L), F32),
        vm((E, E, L), F32),
        vm((3, E, E, L), F32),
        vm((E, E, L), F32),
        vm((3, E + 2, E + 2 * PAD, L), F32),
        vm((2, E, L), F32), vm((E, L), F32), vm((2, 3, E, L), F32), vm((3, E, L), F32),
        vm((2, E, L), F32), vm((E, L), F32), vm((2, 3, E, L), F32), vm((3, E, L), F32),
        dma((T,)), dma((T,)), dma, dma((C,)), dma((C,)),
        dma((C, ns)), dma((C, ns)), dma((C, ns)), dma((C, ns)),
        dma((C, T)), dma((C, T)), dma((5,)), dma((5,)), dma((5,)), dma((5,)),
        vm((E, E, L), BF16), vm((E, E, L), BF16), dma((2,)),
    ]
    return pl.pallas_call(
        functools.partial(kernel, T, Z),
        out_shape=jax.ShapeDtypeStruct((3,) + frame_one.shape, F32),
        in_specs=[pl.BlockSpec(memory_space=pltpu.HBM)] * 2 + [pl.BlockSpec(memory_space=pltpu.VMEM)],
        out_specs=pl.BlockSpec(memory_space=pltpu.VMEM),
        scratch_shapes=scratch,
        compiler_params=pltpu.CompilerParams(
            collective_id=0, has_side_effects=True, vmem_limit_bytes=40 * 1024 * 1024),
        cost_estimate=pl.CostEstimate(flops=131072 * 60, bytes_accessed=2 << 20, transcendentals=0),
        name="warp_flow",
    )(frame_one, frame_two, own)


def solution(mesh):
    spec = P(("groups", "depth"), "tile", "gx")
    vec = P(None, ("groups", "depth"), "tile", "gx")
    body = functools.partial(local, mesh.shape["tile"], mesh.shape["depth"])
    return jax.shard_map(body, mesh=mesh, in_specs=(spec, spec, vec), out_specs=vec, check_vma=False)
```

```python
import functools

import jax
import jax.numpy as jnp
from jax import lax
from jax.experimental import pallas as pl
from jax.experimental.pallas import tpu as pltpu
from jax.sharding import PartitionSpec as P

MESH = pl.DeviceIdType.MESH
F32 = jnp.float32
BF16 = jnp.bfloat16
E = 32
L = 128
NB = 4
CAP = 2
PK = 8
PAD = 8
CHUNKS = 2


def regroup(rows, lane):
    a, b, c, d = rows
    low = lane < 64
    r64 = lambda v: pltpu.roll(v, 64, 1)
    a, c = jnp.where(low, a, r64(c)), jnp.where(low, r64(a), c)
    b, d = jnp.where(low, b, r64(d)), jnp.where(low, r64(b), d)
    even = lax.rem(lane, 64) < 32
    a, b = (jnp.where(even, a, pltpu.roll(b, 32, 1)), jnp.where(even, pltpu.roll(a, 96, 1), b))
    c, d = (jnp.where(even, c, pltpu.roll(d, 32, 1)), jnp.where(even, pltpu.roll(c, 96, 1), d))
    return [a, b, c, d]


def kernel(T, Z, f1_hbm, f2_hbm, sh, out, *scr):
    C = CHUNKS
    S, scr = scr[:C], scr[C:]
    A, scr = scr[:C], scr[C:]
    (B, shr, shs, brp, chs, g, inv, v1p, yb, xb, yv, xv, ybs, xbs, yvs, xvs,
     sem_sh_s, sem_sh_r, sem_loc, sem_gx_s, sem_gx_r, sem_d_s, sem_d_r, sem_f_s, sem_f_r,
     sem_t_s, sem_t_r, sem_h_s, sem_h_r, sem_v_s, sem_v_r, f1, f2, sem_in) = scr
    in2 = pltpu.make_async_copy(f2_hbm, f2, sem_in.at[0])
    in2.start()
    in1 = pltpu.make_async_copy(f1_hbm, f1, sem_in.at[1])
    in1.start()
    CP = PK // C
    m = lax.axis_index("tile")
    z = lax.axis_index("depth")
    x = lax.axis_index("gx")
    px = 1 - x
    nslots = min(Z, 3)
    steps = {1: [], 2: [1]}.get(Z, [1, Z - 1])

    def rcopy(src, dst, ss, rs, dev):
        return pltpu.make_async_remote_copy(
            src_ref=src, dst_ref=dst, send_sem=ss, recv_sem=rs, device_id=dev, device_id_type=MESH)

    barrier = pltpu.get_barrier_semaphore()
    for o in range(1, T):
        pl.semaphore_signal(barrier, inc=1, device_id={"tile": lax.rem(m + o, T)}, device_id_type=MESH)
    for st in steps:
        pl.semaphore_signal(barrier, inc=1, device_id={"depth": lax.rem(z + st, Z)}, device_id_type=MESH)
    pl.semaphore_signal(barrier, inc=1, device_id={"gx": px}, device_id_type=MESH)

    lane = lax.broadcasted_iota(jnp.int32, (E, L), 1)

    in2.wait()
    for c in range(C):
        def pack(zz, carry, c=c):
            rows = [f2[c * CP + zz + PK * q].astype(F32) for q in range(NB)]
            for b, v in enumerate(regroup(rows, lane)):
                S[c][b, zz] = v.astype(BF16)
            return carry
        lax.fori_loop(0, CP, pack, 0)
    shr[m] = sh[...]

    pl.semaphore_wait(barrier, T - 1 + len(steps) + 1)

    sh_cp = []
    for o in range(1, T):
        t = lax.rem(m + o, T)
        cp = rcopy(sh, shr.at[m], sem_sh_s.at[o], sem_sh_r.at[o], {"tile": t})
        cp.start()
        sh_cp.append(cp)

    gx_cp, d_cp = [], []
    for c in range(C):
        own = S[c].at[pl.ds(0, NB)]
        dl = []
        for k, st in enumerate(steps):
            slot = 1 + (k if Z == 2 else 1 - k)
            cp = rcopy(own, S[c].at[pl.ds(slot * 2 * NB, NB)], sem_d_s.at[c, k], sem_d_r.at[c, k],
                       {"depth": lax.rem(z + st, Z)})
            cp.start()
            dl.append((cp, slot))
        d_cp.append(dl)
    for c in range(C):
        cp = rcopy(S[c].at[pl.ds(0, NB)], S[c].at[pl.ds(NB, NB)], sem_gx_s.at[c], sem_gx_r.at[c], {"gx": px})
        cp.start()
        gx_cp.append(cp)

    for cp in sh_cp:
        cp.wait_recv()
    loc = pltpu.make_async_copy(shr, shs, sem_loc)
    loc.start()
    loc.wait()

    def sources(t):
        tiles = [lax.rem(t + shs[t, 1, b], T) for b in range(NB)]
        ranks = []
        for b in range(NB):
            r = jnp.int32(0)
            for e in range(b):
                r = r + jnp.where(tiles[e] == tiles[b], 1, 0)
            ranks.append(r)
        return tiles, ranks

    def rows_for(t):
        tiles, ranks = sources(t)
        picked = [jnp.int32(0)] * CAP
        for b in range(NB):
            s0 = shs[t, 0, b]
            if Z == 1:
                slot = jnp.int32(0)
            elif Z == 2:
                slot = s0 * s0
            else:
                slot = jnp.where(s0 < 0, 2, s0)
            row = slot * (2 * NB) + lax.rem(b + shs[t, 2, b], 2 * NB)
            for k in range(CAP):
                hit = (tiles[b] == m) & (ranks[b] == k)
                picked[k] = picked[k] + jnp.where(hit, row, 0)
        return picked

    want = [rows_for(lax.rem(m + o, T)) for o in range(T)]

    f_cp = []
    t_cp = []
    for c in range(C):
        gx_cp[c].wait_recv()
        fl = []
        for k, (cp, slot) in enumerate(d_cp[c]):
            cp.wait_recv()
            at = slot * 2 * NB
            f = rcopy(S[c].at[pl.ds(at, NB)], S[c].at[pl.ds(at + NB, NB)],
                      sem_f_s.at[c, k], sem_f_r.at[c, k], {"gx": px})
            f.start()
            fl.append(f)
        for f in fl:
            f.wait_recv()
        f_cp.append(fl)
        tl = []
        for o in list(range(1, T)) + [0]:
            t = lax.rem(m + o, T)
            for k in range(CAP):
                row = want[o][k]

                def cut(zz, carry, c=c, o=o, k=k, row=row):
                    if o == 0:
                        A[c][m * CAP + k, zz] = S[c][row, zz]
                    else:
                        B[c, o, k, zz] = S[c][row, zz]
                    return carry
                lax.fori_loop(0, CP, cut, 0)
            if o:
                cp = rcopy(B.at[c, o], A[c].at[pl.ds(m * CAP, CAP)], sem_t_s.at[c, o], sem_t_r.at[c, o], {"tile": t})
                cp.start()
                tl.append(cp)
        t_cp.append(tl)

    tiles, ranks = sources(m)
    pick = [tiles[b] * CAP + jnp.minimum(ranks[b], CAP - 1) for b in range(NB)]
    src_lane = jnp.where(x == 0, L - 1, 0)
    body = pl.ds(PAD, E)
    in1.wait()

    def face_start(c, lo_src, hi_src, lo_dst, hi_dst, ys, yr, xs, xr, ss, rs):
        plan = [
            (ys.at[c, 1], yr.at[c, 0], m < T - 1, m > 0, {"tile": jnp.minimum(m + 1, T - 1)}),
            (ys.at[c, 0], yr.at[c, 1], m > 0, m < T - 1, {"tile": jnp.maximum(m - 1, 0)}),
        ]
        if c == 0:
            plan.append((lo_src, hi_dst, z > 0, z < Z - 1, {"depth": jnp.maximum(z - 1, 0)}))
        if c == C - 1:
            plan.append((hi_src, lo_dst, z < Z - 1, z > 0, {"depth": jnp.minimum(z + 1, Z - 1)}))
        cx = rcopy(xs.at[c], xr.at[c], ss.at[c, 4], rs.at[c, 4], {"gx": px})
        todo = []
        for i, (src, dst, has_to, has_from, dev) in enumerate(plan):
            cp = rcopy(src, dst, ss.at[c, i], rs.at[c, i], dev)

            @pl.when(has_to)
            def _():
                cp.start()

            @pl.when(jnp.logical_not(has_from))
            def _():
                dst[...] = jnp.zeros(dst.shape, F32)
            todo.append((cp, has_to, has_from))
        cx.start()

        def wait_recv():
            for cp, has_to, has_from in todo:
                @pl.when(has_from)
                def _():
                    cp.wait_recv()
            cx.wait_recv()

        def wait_send():
            for cp, has_to, has_from in todo:
                @pl.when(has_to)
                def _():
                    cp.wait_send()
            cx.wait_send()
        return wait_recv, wait_send

    w_b, w_v = [], []
    for c in range(C):
        for cp in t_cp[c]:
            cp.wait_recv()
        xbs[c] = jnp.zeros((E, L), F32)

        def unpack(zz, carry, c=c):
            rows = [A[c][pick[b], zz].astype(F32) for b in range(NB)]
            acc = xbs[c]
            for q, w in enumerate(regroup(rows, lane)):
                zi = c * CP + zz + PK * q
                pos = zz + CP * q
                one = f1[zi].astype(F32)
                br = 0.5 * (one + w)
                brp[zi + 1, body] = br
                chs[zi] = w - one
                ybs[c, 0, pl.ds(pos, 1)] = br[0:1]
                ybs[c, 1, pl.ds(pos, 1)] = br[E - 1:E]
                acc = jnp.where(lane == pos, pltpu.roll(br, lax.rem(pos - src_lane + L, L), 1), acc)
            xbs[c] = acc
            return carry
        lax.fori_loop(0, CP, unpack, 0)
        w_b.append(face_start(c, brp.at[1, body], brp.at[E, body], brp.at[0, body], brp.at[E + 1, body],
                              ybs, yb, xbs, xb, sem_h_s, sem_h_r))

    is0 = jnp.where(x == 0, 1.0, 0.0).astype(F32)
    is1 = 1.0 - is0

    def x_pair(v, halo):
        nxt = jnp.where(lane == L - 1, halo * is0, pltpu.roll(v, L - 1, 1))
        prv = jnp.where(lane == 0, halo * is1, pltpu.roll(v, 1, 1))
        return nxt, prv

    def first(q, carry, c):
        for zz in range(CP):
            zi, pos = c * CP + zz + PK * q, zz + CP * q
            brp[zi + 1, pl.ds(PAD - 1, 1)] = yb[c, 0, pl.ds(pos, 1)]
            brp[zi + 1, pl.ds(PAD + E, 1)] = yb[c, 1, pl.ds(pos, 1)]
        xh = xb[c]
        acc = [xvs[c, i] for i in range(3)]
        for zz in range(CP):
            zi, pos = c * CP + zz + PK * q, zz + CP * q
            gz = 0.5 * (brp[zi + 2, body] - brp[zi, body])
            gy = 0.5 * (brp[zi + 1, pl.ds(PAD + 1, E)] - brp[zi + 1, pl.ds(PAD - 1, E)])
            nxt, prv = x_pair(brp[zi + 1, body], pltpu.roll(xh, lax.rem(src_lane - pos + L, L), 1))
            gx = 0.5 * (nxt - prv)
            iv = 1.0 / (1.0 + gz * gz + gy * gy + gx * gx)
            res = chs[zi] * iv
            inv[zi] = iv
            move = lax.rem(pos - src_lane + L, L)
            for i, gg in enumerate((gz, gy, gx)):
                g[i, zi] = gg
                v = -gg * res
                v1p[i, zi + 1, body] = v
                yvs[c, 0, i, pl.ds(pos, 1)] = v[0:1]
                yvs[c, 1, i, pl.ds(pos, 1)] = v[E - 1:E]
                acc[i] = jnp.where(lane == pos, pltpu.roll(v, move, 1), acc[i])
        for i in range(3):
            xvs[c, i] = acc[i]
        return carry

    three = pl.ds(0, 3)
    xvs[...] = jnp.zeros(xvs.shape, F32)
    for c in range(C):
        if c == 0:
            w_b[c][0]()
            lax.fori_loop(1, NB, functools.partial(first, c=c), 0)
            for later in range(1, C):
                w_b[later][0]()
            lax.fori_loop(0, 1, functools.partial(first, c=c), 0)
        else:
            lax.fori_loop(0, NB, functools.partial(first, c=c), 0)
        w_v.append(face_start(c, v1p.at[three, 1, body], v1p.at[three, E, body], v1p.at[three, 0, body],
                              v1p.at[three, E + 1, body], yvs, yv, xvs, xv, sem_v_s, sem_v_r))

    def second(q, carry, c):
        for zz in range(CP):
            zi, pos = c * CP + zz + PK * q, zz + CP * q
            for i in range(3):
                v1p[i, zi + 1, pl.ds(PAD - 1, 1)] = yv[c, 0, i, pl.ds(pos, 1)]
                v1p[i, zi + 1, pl.ds(PAD + E, 1)] = yv[c, 1, i, pl.ds(pos, 1)]
        for zz in range(CP):
            zi, pos = c * CP + zz + PK * q, zz + CP * q
            back = lax.rem(src_lane - pos + L, L)
            avg = []
            for i in range(3):
                nxt, prv = x_pair(v1p[i, zi + 1, body], pltpu.roll(xv[c, i], back, 1))
                total = (v1p[i, zi + 2, body] + v1p[i, zi, body]
                         + v1p[i, zi + 1, pl.ds(PAD + 1, E)] + v1p[i, zi + 1, pl.ds(PAD - 1, E)] + nxt + prv)
                avg.append(total * (1.0 / 6.0))
            gs = [g[i, zi] for i in range(3)]
            res = (gs[0] * avg[0] + gs[1] * avg[1] + gs[2] * avg[2] + chs[zi]) * inv[zi]
            for i in range(3):
                out[i, zi] = avg[i] - gs[i] * res
        return carry

    w_v[0][0]()
    lax.fori_loop(1, NB, functools.partial(second, c=0), 0)
    for c in range(1, C):
        w_v[c][0]()
    lax.fori_loop(0, 1, functools.partial(second, c=0), 0)
    for c in range(1, C):
        lax.fori_loop(0, NB, functools.partial(second, c=c), 0)

    for cp in sh_cp:
        cp.wait_send()
    for c in range(C):
        gx_cp[c].wait_send()
        for cp, slot in d_cp[c]:
            cp.wait_send()
        for cp in f_cp[c]:
            cp.wait_send()
        for cp in t_cp[c]:
            cp.wait_send()
    for c in range(C):
        w_b[c][1]()
        w_v[c][1]()


def local(T, Z, frame_one, frame_two, shifts):
    C = CHUNKS
    CP = PK // C
    own = jnp.pad(shifts.reshape(3, NB), ((0, 5), (0, L - NB)))
    nslots = min(Z, 3)
    dma = pltpu.SemaphoreType.DMA
    ns = max(1, nslots - 1)
    vm = pltpu.VMEM
    scratch = [vm((nslots * 2 * NB, CP, E, L), BF16) for _ in range(C)]
    scratch += [vm((T * CAP, CP, E, L), BF16) for _ in range(C)]
    scratch += [
        vm((C, T, CAP, CP, E, L), BF16),
        vm((T, 8, L), jnp.int32),
        pltpu.SMEM((T, 8, L), jnp.int32),
        vm((E + 2, E + 2 * PAD, L), F32),
        vm((E, E, L), F32),
        vm((3, E, E, L), F32),
        vm((E, E, L), F32),
        vm((3, E + 2, E + 2 * PAD, L), F32),
        vm((C, 2, E // C, L), F32), vm((C, E, L), F32), vm((C, 2, 3, E // C, L), F32), vm((C, 3, E, L), F32),
        vm((C, 2, E // C, L), F32), vm((C, E, L), F32), vm((C, 2, 3, E // C, L), F32), vm((C, 3, E, L), F32),
        dma((T,)), dma((T,)), dma, dma((C,)), dma((C,)),
        dma((C, ns)), dma((C, ns)), dma((C, ns)), dma((C, ns)),
        dma((C, T)), dma((C, T)), dma((C, 5)), dma((C, 5)), dma((C, 5)), dma((C, 5)),
        vm((E, E, L), BF16), vm((E, E, L), BF16), dma((2,)),
    ]
    return pl.pallas_call(
        functools.partial(kernel, T, Z),
        out_shape=jax.ShapeDtypeStruct((3,) + frame_one.shape, F32),
        in_specs=[pl.BlockSpec(memory_space=pltpu.HBM)] * 2 + [pl.BlockSpec(memory_space=pltpu.VMEM)],
        out_specs=pl.BlockSpec(memory_space=pltpu.VMEM),
        scratch_shapes=scratch,
        compiler_params=pltpu.CompilerParams(
            collective_id=0, has_side_effects=True, vmem_limit_bytes=40 * 1024 * 1024),
        cost_estimate=pl.CostEstimate(flops=131072 * 60, bytes_accessed=2 << 20, transcendentals=0),
        name="warp_flow",
    )(frame_one, frame_two, own)


def solution(mesh):
    spec = P(("groups", "depth"), "tile", "gx")
    vec = P(None, ("groups", "depth"), "tile", "gx")
    body = functools.partial(local, mesh.shape["tile"], mesh.shape["depth"])
    return jax.shard_map(body, mesh=mesh, in_specs=(spec, spec, vec), out_specs=vec, check_vma=False)
```

```python
import functools

import jax
import jax.numpy as jnp
from jax import lax
from jax.experimental import pallas as pl
from jax.experimental.pallas import tpu as pltpu
from jax.sharding import PartitionSpec as P

MESH = pl.DeviceIdType.MESH
F32 = jnp.float32
BF16 = jnp.bfloat16
E = 32
L = 128
NB = 4
CAP = 2
PK = 8
PAD = 8
CHUNKS = 4
FACE_CHUNKS = 2


def regroup(rows, lane):
    a, b, c, d = rows
    low = lane < 64
    r64 = lambda v: pltpu.roll(v, 64, 1)
    a, c = jnp.where(low, a, r64(c)), jnp.where(low, r64(a), c)
    b, d = jnp.where(low, b, r64(d)), jnp.where(low, r64(b), d)
    even = lax.rem(lane, 64) < 32
    a, b = (jnp.where(even, a, pltpu.roll(b, 32, 1)), jnp.where(even, pltpu.roll(a, 96, 1), b))
    c, d = (jnp.where(even, c, pltpu.roll(d, 32, 1)), jnp.where(even, pltpu.roll(c, 96, 1), d))
    return [a, b, c, d]


def kernel(T, Z, f1, f2, sh, out, *scr):
    C = CHUNKS
    S, scr = scr[:C], scr[C:]
    A, scr = scr[:C], scr[C:]
    (B, shr, shs, brp, chs, g, inv, v1p, yb, xb, yv, xv, ybs, xbs, yvs, xvs,
     sem_sh_s, sem_sh_r, sem_loc, sem_gx_s, sem_gx_r, sem_d_s, sem_d_r, sem_f_s, sem_f_r,
     sem_t_s, sem_t_r, sem_h_s, sem_h_r, sem_v_s, sem_v_r) = scr
    CP = PK // C
    H = FACE_CHUNKS
    FP = PK // H
    m = lax.axis_index("tile")
    z = lax.axis_index("depth")
    x = lax.axis_index("gx")
    px = 1 - x
    nslots = min(Z, 3)
    steps = {1: [], 2: [1]}.get(Z, [1, Z - 1])

    def rcopy(src, dst, ss, rs, dev):
        return pltpu.make_async_remote_copy(
            src_ref=src, dst_ref=dst, send_sem=ss, recv_sem=rs, device_id=dev, device_id_type=MESH)

    barrier = pltpu.get_barrier_semaphore()
    for o in range(1, T):
        pl.semaphore_signal(barrier, inc=1, device_id={"tile": lax.rem(m + o, T)}, device_id_type=MESH)
    for st in steps:
        pl.semaphore_signal(barrier, inc=1, device_id={"depth": lax.rem(z + st, Z)}, device_id_type=MESH)
    pl.semaphore_signal(barrier, inc=1, device_id={"gx": px}, device_id_type=MESH)

    lane = lax.broadcasted_iota(jnp.int32, (E, L), 1)

    for c in range(C):
        def pack(zz, carry, c=c):
            rows = [f2[c * CP + zz + PK * q].astype(F32) for q in range(NB)]
            for b, v in enumerate(regroup(rows, lane)):
                S[c][b, zz] = v.astype(BF16)
            return carry
        lax.fori_loop(0, CP, pack, 0, unroll=True)
    shr[m] = sh[...]

    pl.semaphore_wait(barrier, T - 1 + len(steps) + 1)

    sh_cp = []
    for o in range(1, T):
        t = lax.rem(m + o, T)
        cp = rcopy(sh, shr.at[m], sem_sh_s.at[o], sem_sh_r.at[o], {"tile": t})
        cp.start()
        sh_cp.append(cp)

    gx_cp, d_cp = [], []
    for c in range(C):
        own = S[c].at[pl.ds(0, NB)]
        dl = []
        for k, st in enumerate(steps):
            slot = 1 + (k if Z == 2 else 1 - k)
            cp = rcopy(own, S[c].at[pl.ds(slot * 2 * NB, NB)], sem_d_s.at[c, k], sem_d_r.at[c, k],
                       {"depth": lax.rem(z + st, Z)})
            cp.start()
            dl.append((cp, slot))
        d_cp.append(dl)
    for c in range(C):
        cp = rcopy(S[c].at[pl.ds(0, NB)], S[c].at[pl.ds(NB, NB)], sem_gx_s.at[c], sem_gx_r.at[c], {"gx": px})
        cp.start()
        gx_cp.append(cp)

    for cp in sh_cp:
        cp.wait_recv()
    loc = pltpu.make_async_copy(shr, shs, sem_loc)
    loc.start()
    loc.wait()

    def sources(t):
        tiles = [lax.rem(t + shs[t, 1, b], T) for b in range(NB)]
        ranks = []
        for b in range(NB):
            r = jnp.int32(0)
            for e in range(b):
                r = r + jnp.where(tiles[e] == tiles[b], 1, 0)
            ranks.append(r)
        return tiles, ranks

    def rows_for(t):
        tiles, ranks = sources(t)
        picked = [jnp.int32(0)] * CAP
        for b in range(NB):
            s0 = shs[t, 0, b]
            if Z == 1:
                slot = jnp.int32(0)
            elif Z == 2:
                slot = s0 * s0
            else:
                slot = jnp.where(s0 < 0, 2, s0)
            row = slot * (2 * NB) + lax.rem(b + shs[t, 2, b], 2 * NB)
            for k in range(CAP):
                hit = (tiles[b] == m) & (ranks[b] == k)
                picked[k] = picked[k] + jnp.where(hit, row, 0)
        return picked

    want = [rows_for(lax.rem(m + o, T)) for o in range(T)]

    f_cp = []
    t_cp = []
    for c in range(C):
        gx_cp[c].wait_recv()
        fl = []
        for k, (cp, slot) in enumerate(d_cp[c]):
            cp.wait_recv()
            at = slot * 2 * NB
            f = rcopy(S[c].at[pl.ds(at, NB)], S[c].at[pl.ds(at + NB, NB)],
                      sem_f_s.at[c, k], sem_f_r.at[c, k], {"gx": px})
            f.start()
            fl.append(f)
        for f in fl:
            f.wait_recv()
        f_cp.append(fl)
        tl = []
        for o in [T // 2] + [o for o in range(1, T) if o != T // 2] + [0]:
            t = lax.rem(m + o, T)
            for k in range(CAP):
                row = want[o][k]

                def cut(zz, carry, c=c, o=o, k=k, row=row):
                    if o == 0:
                        A[c][m * CAP + k, zz] = S[c][row, zz]
                    else:
                        B[c, o, k, zz] = S[c][row, zz]
                    return carry
                lax.fori_loop(0, CP, cut, 0, unroll=True)
            if o:
                cp = rcopy(B.at[c, o], A[c].at[pl.ds(m * CAP, CAP)], sem_t_s.at[c, o], sem_t_r.at[c, o], {"tile": t})
                cp.start()
                tl.append(cp)
        t_cp.append(tl)

    tiles, ranks = sources(m)
    pick = [tiles[b] * CAP + jnp.minimum(ranks[b], CAP - 1) for b in range(NB)]
    src_lane = jnp.where(x == 0, L - 1, 0)
    body = pl.ds(PAD, E)

    def face_start(c, lo_src, hi_src, lo_dst, hi_dst, ys, yr, xs, xr, ss, rs):
        plan = [
            (ys.at[c, 1], yr.at[c, 0], m < T - 1, m > 0, {"tile": jnp.minimum(m + 1, T - 1)}),
            (ys.at[c, 0], yr.at[c, 1], m > 0, m < T - 1, {"tile": jnp.maximum(m - 1, 0)}),
        ]
        if c == 0:
            plan.append((lo_src, hi_dst, z > 0, z < Z - 1, {"depth": jnp.maximum(z - 1, 0)}))
        if c == H - 1:
            plan.append((hi_src, lo_dst, z < Z - 1, z > 0, {"depth": jnp.minimum(z + 1, Z - 1)}))
        cx = rcopy(xs.at[c], xr.at[c], ss.at[c, 4], rs.at[c, 4], {"gx": px})
        todo = []
        for i, (src, dst, has_to, has_from, dev) in enumerate(plan):
            cp = rcopy(src, dst, ss.at[c, i], rs.at[c, i], dev)

            @pl.when(has_to)
            def _():
                cp.start()

            @pl.when(jnp.logical_not(has_from))
            def _():
                dst[...] = jnp.zeros(dst.shape, F32)
            todo.append((cp, has_to, has_from))
        cx.start()

        def wait_recv():
            for cp, has_to, has_from in todo:
                @pl.when(has_from)
                def _():
                    cp.wait_recv()
            cx.wait_recv()

        def wait_send():
            for cp, has_to, has_from in todo:
                @pl.when(has_to)
                def _():
                    cp.wait_send()
            cx.wait_send()
        return wait_recv, wait_send

    w_b, w_v = [], []
    for h in range(H):
        xbs[h] = jnp.zeros((E, L), F32)
        for c in range(h * C // H, (h + 1) * C // H):
            for cp in t_cp[c]:
                cp.wait_recv()

            def unpack(zz, carry, c=c, h=h):
                rows = [A[c][pick[b], zz].astype(F32) for b in range(NB)]
                acc = xbs[h]
                for q, w in enumerate(regroup(rows, lane)):
                    zi = c * CP + zz + PK * q
                    pos = c * CP - h * FP + zz + FP * q
                    one = f1[zi].astype(F32)
                    br = 0.5 * (one + w)
                    brp[zi + 1, body] = br
                    chs[zi] = w - one
                    ybs[h, 0, pl.ds(pos, 1)] = br[0:1]
                    ybs[h, 1, pl.ds(pos, 1)] = br[E - 1:E]
                    acc = jnp.where(lane == pos, pltpu.roll(br, lax.rem(pos - src_lane + L, L), 1), acc)
                xbs[h] = acc
                return carry
            lax.fori_loop(0, CP, unpack, 0, unroll=True)
        w_b.append(face_start(h, brp.at[1, body], brp.at[E, body], brp.at[0, body], brp.at[E + 1, body],
                              ybs, yb, xbs, xb, sem_h_s, sem_h_r))

    is0 = jnp.where(x == 0, 1.0, 0.0).astype(F32)
    is1 = 1.0 - is0

    def x_pair(v, halo):
        nxt = jnp.where(lane == L - 1, halo * is0, pltpu.roll(v, L - 1, 1))
        prv = jnp.where(lane == 0, halo * is1, pltpu.roll(v, 1, 1))
        return nxt, prv

    def first(q, carry, c):
        for zz in range(FP):
            zi, pos = c * FP + zz + PK * q, zz + FP * q
            brp[zi + 1, pl.ds(PAD - 1, 1)] = yb[c, 0, pl.ds(pos, 1)]
            brp[zi + 1, pl.ds(PAD + E, 1)] = yb[c, 1, pl.ds(pos, 1)]
        xh = xb[c]
        acc = [xvs[c, i] for i in range(3)]
        for zz in range(FP):
            zi, pos = c * FP + zz + PK * q, zz + FP * q
            gz = 0.5 * (brp[zi + 2, body] - brp[zi, body])
            gy = 0.5 * (brp[zi + 1, pl.ds(PAD + 1, E)] - brp[zi + 1, pl.ds(PAD - 1, E)])
            nxt, prv = x_pair(brp[zi + 1, body], pltpu.roll(xh, lax.rem(src_lane - pos + L, L), 1))
            gx = 0.5 * (nxt - prv)
            iv = 1.0 / (1.0 + gz * gz + gy * gy + gx * gx)
            res = chs[zi] * iv
            inv[zi] = iv
            move = lax.rem(pos - src_lane + L, L)
            for i, gg in enumerate((gz, gy, gx)):
                g[i, zi] = gg
                v = -gg * res
                v1p[i, zi + 1, body] = v
                yvs[c, 0, i, pl.ds(pos, 1)] = v[0:1]
                yvs[c, 1, i, pl.ds(pos, 1)] = v[E - 1:E]
                acc[i] = jnp.where(lane == pos, pltpu.roll(v, move, 1), acc[i])
        for i in range(3):
            xvs[c, i] = acc[i]
        return carry

    three = pl.ds(0, 3)
    xvs[...] = jnp.zeros(xvs.shape, F32)
    for c in range(H):
        if c == 0:
            w_b[c][0]()
            lax.fori_loop(1, NB, functools.partial(first, c=c), 0)
            for later in range(1, H):
                w_b[later][0]()
            lax.fori_loop(0, 1, functools.partial(first, c=c), 0)
        else:
            lax.fori_loop(0, NB, functools.partial(first, c=c), 0)
        w_v.append(face_start(c, v1p.at[three, 1, body], v1p.at[three, E, body], v1p.at[three, 0, body],
                              v1p.at[three, E + 1, body], yvs, yv, xvs, xv, sem_v_s, sem_v_r))

    def second(q, carry, c):
        for zz in range(FP):
            zi, pos = c * FP + zz + PK * q, zz + FP * q
            for i in range(3):
                v1p[i, zi + 1, pl.ds(PAD - 1, 1)] = yv[c, 0, i, pl.ds(pos, 1)]
                v1p[i, zi + 1, pl.ds(PAD + E, 1)] = yv[c, 1, i, pl.ds(pos, 1)]
        for zz in range(FP):
            zi, pos = c * FP + zz + PK * q, zz + FP * q
            back = lax.rem(src_lane - pos + L, L)
            avg = []
            for i in range(3):
                nxt, prv = x_pair(v1p[i, zi + 1, body], pltpu.roll(xv[c, i], back, 1))
                total = (v1p[i, zi + 2, body] + v1p[i, zi, body]
                         + v1p[i, zi + 1, pl.ds(PAD + 1, E)] + v1p[i, zi + 1, pl.ds(PAD - 1, E)] + nxt + prv)
                avg.append(total * (1.0 / 6.0))
            gs = [g[i, zi] for i in range(3)]
            res = (gs[0] * avg[0] + gs[1] * avg[1] + gs[2] * avg[2] + chs[zi]) * inv[zi]
            for i in range(3):
                out[i, zi] = avg[i] - gs[i] * res
        return carry

    w_v[0][0]()
    lax.fori_loop(1, NB, functools.partial(second, c=0), 0)
    for c in range(1, H):
        w_v[c][0]()
    lax.fori_loop(0, 1, functools.partial(second, c=0), 0)
    for c in range(1, H):
        lax.fori_loop(0, NB, functools.partial(second, c=c), 0)

    for cp in sh_cp:
        cp.wait_send()
    for c in range(C):
        gx_cp[c].wait_send()
        for cp, slot in d_cp[c]:
            cp.wait_send()
        for cp in f_cp[c]:
            cp.wait_send()
        for cp in t_cp[c]:
            cp.wait_send()
    for h in range(H):
        w_b[h][1]()
        w_v[h][1]()


def local(T, Z, frame_one, frame_two, shifts):
    C, H = CHUNKS, FACE_CHUNKS
    CP = PK // C
    own = jnp.pad(shifts.reshape(3, NB), ((0, 5), (0, L - NB)))
    nslots = min(Z, 3)
    dma = pltpu.SemaphoreType.DMA
    ns = max(1, nslots - 1)
    vm = pltpu.VMEM
    scratch = [vm((nslots * 2 * NB, CP, E, L), BF16) for _ in range(C)]
    scratch += [vm((T * CAP, CP, E, L), BF16) for _ in range(C)]
    scratch += [
        vm((C, T, CAP, CP, E, L), BF16),
        vm((T, 8, L), jnp.int32),
        pltpu.SMEM((T, 8, L), jnp.int32),
        vm((E + 2, E + 2 * PAD, L), F32),
        vm((E, E, L), F32),
        vm((3, E, E, L), F32),
        vm((E, E, L), F32),
        vm((3, E + 2, E + 2 * PAD, L), F32),
        vm((H, 2, E // H, L), F32), vm((H, E, L), F32), vm((H, 2, 3, E // H, L), F32), vm((H, 3, E, L), F32),
        vm((H, 2, E // H, L), F32), vm((H, E, L), F32), vm((H, 2, 3, E // H, L), F32), vm((H, 3, E, L), F32),
        dma((T,)), dma((T,)), dma, dma((C,)), dma((C,)),
        dma((C, ns)), dma((C, ns)), dma((C, ns)), dma((C, ns)),
        dma((C, T)), dma((C, T)), dma((H, 5)), dma((H, 5)), dma((H, 5)), dma((H, 5)),

    ]
    return pl.pallas_call(
        functools.partial(kernel, T, Z),
        out_shape=jax.ShapeDtypeStruct((3,) + frame_one.shape, F32),
        in_specs=[pl.BlockSpec(memory_space=pltpu.VMEM)] * 3,
        out_specs=pl.BlockSpec(memory_space=pltpu.VMEM),
        scratch_shapes=scratch,
        compiler_params=pltpu.CompilerParams(
            collective_id=0, has_side_effects=True, vmem_limit_bytes=40 * 1024 * 1024),
        cost_estimate=pl.CostEstimate(flops=131072 * 60, bytes_accessed=2 << 20, transcendentals=0),
        name="warp_flow",
    )(frame_one, frame_two, own)


def solution(mesh):
    spec = P(("groups", "depth"), "tile", "gx")
    vec = P(None, ("groups", "depth"), "tile", "gx")
    body = functools.partial(local, mesh.shape["tile"], mesh.shape["depth"])
    return jax.shard_map(body, mesh=mesh, in_specs=(spec, spec, vec), out_specs=vec, check_vma=False)
```
